128 devices in a mesh: ctx: 32 (over x, z, core), tp: 4 (over y).
Axes of the slice: x: 4, y: 4, z: 4, core: 2. Of those that a mesh axis runs over, the one named last changes fastest.
Arguments:
- queries: bfloat16 [16384, 4096], P('ctx', 'tp'), may hold values from -160 to 160
- slot_table: int32 [256, 4], P('ctx'), may hold values from -1 to 831, as said below
- states: bfloat16 [832, 128, 512], P('ctx'), may hold values from -6 to 6
- key_weight: bfloat16 [512, 4096], P(None, 'tp'), may hold values from -0.25 to 0.25
- value_weight: bfloat16 [512, 4096], P(None, 'tp'), may hold values from -0.25 to 0.25
- out_grad: bfloat16 [16384, 4096], P('ctx', 'tp'), may hold values from -6 to 6
Outputs:
- attended: bfloat16 [16384, 4096], P('ctx', 'tp')
- query_grad: bfloat16 [16384, 4096], P('ctx', 'tp')
- states_grad: bfloat16 [832, 128, 512], P('ctx', None, 'tp')
- key_weight_grad: float32 [512, 4096], P('ctx', 'tp')
- value_weight_grad: float32 [512, 4096], P('ctx', 'tp')
The draws below stay inside these ranges and needn't reach their ends.
Inputs may be any that keep to these rules, and one draw needn't show every extreme that they name: `slot_table`: row c of the table lists the slots of stretch c's neighbours: 1 to 4 slot numbers first, then -1; one row in every draw has 4. Every slot appears exactly once. Of the neighbours of one device's 8 stretches, at most 2 are stored in the slots of any one device, and that many in some pair of devices in every draw.
All inputs are finite; a program needn't handle non-finite values.
Results may differ from the reference program's by a relative error of at most 0.023.
The reference program's roundings to bfloat16 on the way count: a program that leaves them out, or rounds other values in their place, can miss the bound.
Values may be sent and summed in bfloat16 or wider, within the bound.
No kernel may reach another device: no remote copies, remote signals or barrier semaphores. Data moves between devices by JAX's collectives and lax.ppermute only.
A program may use at most 192 MiB of HBM per device.

```python
import jax
import jax.numpy as jnp
from jax import lax

HEADS = 32
HEAD_DIM = 128
D_ENC = 512
STRETCH = 64
NLEN = 128
KMAX = 4
CAP = 2
SLOTS_DEV = 26
STRETCHES = 256
TOKENS = 16384
SLOTS = 832
N_CTX = 32
N_TP = 4


def draw_queries(key, part):
    key = jax.random.fold_in(key, 3)
    base = jnp.clip(jax.random.normal(key, (TOKENS, HEADS * HEAD_DIM), jnp.float32), -4.0, 4.0)
    return base.astype(jnp.bfloat16)


def draw_slot_table(key, part):
    key = jax.random.fold_in(key, 7)
    base = jax.random.randint(jax.random.fold_in(key, 11), (STRETCHES,), 0, 1 << 15)
    leader = jax.random.randint(jax.random.fold_in(key, 12), (), 0, STRETCHES)
    base = jnp.where(jnp.arange(STRETCHES) == leader, 1 << 19, base)
    levels = jnp.arange(1, KMAX)
    score = (base[:, None] - levels[None, :] * 20000) * (KMAX * STRETCHES)
    score = score + jnp.arange(STRETCHES)[:, None] * (KMAX - 1) + levels[None, :] - 1
    extra = SLOTS - STRETCHES
    chosen = lax_top(score.reshape(-1), extra)
    owners_of = chosen // (KMAX - 1)
    counts = 1 + jnp.sum((owners_of[:, None] == jnp.arange(STRETCHES)[None, :]).astype(jnp.int32), axis=0)
    start = jnp.cumsum(counts) - counts
    ranks = start[:, None] + jnp.arange(KMAX)[None, :]
    group = ranks // CAP
    order = jax.random.permutation(jax.random.fold_in(key, 13), N_CTX)
    owner = order[group % N_CTX]
    position = group // N_CTX * CAP + ranks % CAP
    live = jnp.arange(KMAX)[None, :] < counts[:, None]
    return jnp.where(live, owner * SLOTS_DEV + position, -1).astype(jnp.int32)


def lax_top(values, count):
    return jax.lax.top_k(values, count)[1]


def steps_of(key, extent, split, low, top_value):
    def one(dim, blocks):
        draws = jax.random.uniform(jax.random.fold_in(jax.random.fold_in(key, 6), dim), (blocks,), jnp.float32, low / len(split), top_value / len(split))
        return jnp.repeat(jnp.exp(draws), extent[dim] // blocks).reshape((-1,) + (1,) * (len(extent) - dim - 1))

    level = one(*split[0])
    for cut in split[1:]:
        level = level * one(*cut)
    return level


def gaussian(stream_key, shape, scale, most, shards=(), held_as=jnp.bfloat16):
    entries = jax.random.normal(stream_key, shape, jnp.float32) * scale
    if len(shards) > 0:
        entries = steps_of(stream_key, shape, shards, -0.22, 0.18) * entries
    return jnp.clip(entries, min=-most, max=most).astype(held_as)


def setup_inputs(seed: int = 0) -> dict:
    splits = jax.random.split(jax.random.key(seed), 7)
    return {
        "queries": draw_queries(jax.random.fold_in(splits[6], 71), 0),
        "slot_table": draw_slot_table(jax.random.fold_in(splits[6], 71), 0),
        "states": gaussian(splits[2], (SLOTS, NLEN, D_ENC), 1.0, 6.0, ((0, 32),)),
        "key_weight": gaussian(splits[3], (D_ENC, HEADS * HEAD_DIM), D_ENC ** -0.5, 0.25, ((1, 4),)),
        "value_weight": gaussian(splits[4], (D_ENC, HEADS * HEAD_DIM), D_ENC ** -0.5, 0.25, ((1, 4),)),
        "out_grad": gaussian(splits[5], (TOKENS, HEADS * HEAD_DIM), 1.0, 6.0, ((0, 32), (1, 4))),
    }


def reference(queries, slot_table, states, key_weight, value_weight, out_grad):
    width = HEADS * HEAD_DIM
    scale = HEAD_DIM ** -0.5
    flat_states = states.reshape(SLOTS * NLEN, D_ENC)
    keys = jnp.dot(flat_states, key_weight, preferred_element_type=jnp.float32).astype(jnp.bfloat16).reshape(SLOTS, NLEN, width)
    values = jnp.dot(flat_states, value_weight, preferred_element_type=jnp.float32).astype(jnp.bfloat16).reshape(SLOTS, NLEN, width)
    present = slot_table >= 0
    safe_slots = jnp.where(present, slot_table, 0).astype(jnp.int32)
    drop_slots = jnp.where(present, slot_table, SLOTS).astype(jnp.int32)
    query_stretches = queries.reshape(STRETCHES, STRETCH, HEADS, HEAD_DIM)
    grad_stretches = out_grad.reshape(STRETCHES, STRETCH, HEADS, HEAD_DIM)

    def stretch_step(carry, inputs):
        key_acc, value_acc = carry
        query, dout, live, take_rows, put_rows = inputs
        stretch_keys = keys[take_rows].reshape(KMAX * NLEN, HEADS, HEAD_DIM).astype(jnp.float32)
        stretch_values = values[take_rows].reshape(KMAX * NLEN, HEADS, HEAD_DIM).astype(jnp.float32)
        query_f = query.astype(jnp.float32)
        dout_f = dout.astype(jnp.float32)
        mask = jnp.repeat(live, NLEN)[None, None, :]
        scores = jnp.einsum('qhd,khd->hqk', query_f, stretch_keys) * scale
        scores = jnp.where(mask, scores, -jnp.inf)
        top = jnp.max(scores, axis=-1, keepdims=True)
        expo = jnp.exp(scores - top)
        probs = expo / jnp.sum(expo, axis=-1, keepdims=True)
        probs_b = probs.astype(jnp.bfloat16)
        attended = jnp.einsum('hqk,khd->qhd', probs_b.astype(jnp.float32), stretch_values).astype(jnp.bfloat16)
        dprobs = jnp.einsum('qhd,khd->hqk', dout_f, stretch_values)
        dscores = probs * (dprobs - jnp.sum(probs * dprobs, axis=-1, keepdims=True))
        dscores_b = dscores.astype(jnp.bfloat16).astype(jnp.float32)
        query_grad = (jnp.einsum('hqk,khd->qhd', dscores_b, stretch_keys) * scale).astype(jnp.bfloat16)
        key_grad = (jnp.einsum('hqk,qhd->khd', dscores_b, query_f) * scale).astype(jnp.bfloat16)
        value_grad = jnp.einsum('hqk,qhd->khd', probs_b.astype(jnp.float32), dout_f).astype(jnp.bfloat16)
        key_acc = key_acc.at[put_rows].set(key_grad.reshape(KMAX, NLEN, width), mode="drop")
        value_acc = value_acc.at[put_rows].set(value_grad.reshape(KMAX, NLEN, width), mode="drop")
        return (key_acc, value_acc), (attended.reshape(STRETCH, width), query_grad.reshape(STRETCH, width))

    start = (jnp.zeros((SLOTS, NLEN, width), jnp.bfloat16), jnp.zeros((SLOTS, NLEN, width), jnp.bfloat16))
    (key_acc, value_acc), (attended, query_grad) = lax.scan(stretch_step, start, (query_stretches, grad_stretches, present, safe_slots, drop_slots))
    attended = attended.reshape(TOKENS, width)
    query_grad = query_grad.reshape(TOKENS, width)
    key_flat = key_acc.reshape(SLOTS * NLEN, width)
    value_flat = value_acc.reshape(SLOTS * NLEN, width)
    key_weight_grad = jnp.dot(flat_states.T, key_flat, preferred_element_type=jnp.float32)
    value_weight_grad = jnp.dot(flat_states.T, value_flat, preferred_element_type=jnp.float32)
    group = width // N_TP
    total = jnp.zeros((SLOTS * NLEN, D_ENC), jnp.float32)
    for number in range(N_TP):
        lower = number * group
        upper = lower + group
        partial_sum = jnp.dot(key_flat[:, lower:upper], key_weight[:, lower:upper].T, preferred_element_type=jnp.float32)
        partial_sum = partial_sum + jnp.dot(value_flat[:, lower:upper], value_weight[:, lower:upper].T, preferred_element_type=jnp.float32)
        rounded = lax.optimization_barrier(partial_sum.astype(jnp.bfloat16))
        total = total + rounded.astype(jnp.float32)
    states_grad = total.astype(jnp.bfloat16).reshape(SLOTS, NLEN, D_ENC)
    return attended, query_grad, states_grad, key_weight_grad, value_weight_grad
```

```python
import functools

import jax
import jax.numpy as jnp
from jax import lax
from jax.experimental import pallas as pl
from jax.experimental.pallas import tpu as pltpu
from jax.sharding import PartitionSpec as P

HEAD_DIM = 128
CHUNK = 4
F32 = jnp.float32
BF16 = jnp.bfloat16
NN = (((1,), (0,)), ((), ()))
NT = (((1,), (1,)), ((), ()))
TN = (((0,), (0,)), ((), ()))
MIB = 2**20


def dot(a, b, dims=NN):
    return lax.dot_general(a, b, dims, preferred_element_type=F32)


def attend_kernel(counts, s0, s1, s2, s3, w, wt, q_ref, do_ref, *rest, heads, span, first):
    att, qg, grads, p0, p1, p2, p3, kv = rest[-8:]
    c = pl.program_id(0)
    width = heads * HEAD_DIM
    scale = HEAD_DIM ** (-0.5)
    rows = s0.shape[0]
    length = q_ref.shape[0]
    states = jnp.concatenate([s0[...], s1[...], s2[...], s3[...]], axis=1)
    kv[...] = dot(states, w[...]).astype(BF16)
    mask = lax.broadcasted_iota(jnp.int32, (rows, 1), 0) < counts[first + c] * span
    zero = jnp.zeros((length, HEAD_DIM), BF16)

    def spread(ref, lo):
        top = jnp.concatenate([ref[:, lo : lo + HEAD_DIM], zero], axis=1)
        low = jnp.concatenate([zero, ref[:, lo + HEAD_DIM : lo + 2 * HEAD_DIM]], axis=1)
        return jnp.concatenate([top, low], axis=0)

    for h in range(0, heads, 2):
        lo = h * HEAD_DIM
        mid, hi = lo + HEAD_DIM, lo + 2 * HEAD_DIM
        q = spread(q_ref, lo)
        do = spread(do_ref, lo)
        k = kv[:, lo:hi]
        v = kv[:, width + lo : width + hi]
        scores = jnp.where(mask, dot(k, q, NT), -jnp.inf)
        dprobs = dot(v, do, NT)
        expo = jnp.exp((scores - jnp.max(scores, axis=0, keepdims=True)) * scale)
        probs = expo * (1.0 / jnp.sum(expo, axis=0, keepdims=True))
        dscores = probs * (dprobs - jnp.sum(probs * dprobs, axis=0, keepdims=True))
        probs_b = probs.astype(BF16)
        dscores_b = dscores.astype(BF16)
        grads[:, width + lo : width + hi] = dot(probs_b, do).astype(BF16)
        grads[:, lo:hi] = (dot(dscores_b, q) * scale).astype(BF16)
        both = dot(probs_b, v, TN).astype(BF16)
        att[:, lo:mid] = both[:length, :HEAD_DIM]
        att[:, mid:hi] = both[length:, HEAD_DIM:]
        both = (dot(dscores_b, k, TN) * scale).astype(BF16)
        qg[:, lo:mid] = both[:length, :HEAD_DIM]
        qg[:, mid:hi] = both[length:, HEAD_DIM:]
    part = dot(grads[...], wt[...]).astype(BF16)
    n = p0.shape[1]
    p0[...] = part[:, :n]
    p1[...] = part[:, n : 2 * n]
    p2[...] = part[:, 2 * n : 3 * n]
    p3[...] = part[:, 3 * n :]


def attend(counts, pieces, w, wt, q, do, after, first, number, span):
    heads = q.shape[1] // HEAD_DIM
    stretches = counts.shape[0]
    length = q.shape[0] // stretches
    width = q.shape[1]
    rows = pieces[0].shape[0] // number
    part = pieces[0].shape[1]
    piece = pl.BlockSpec((rows, part), lambda c, n: (c, 0))
    token = pl.BlockSpec((length, width), lambda c, n: (first + c, 0))
    whole = pl.BlockSpec((rows, 2 * width), lambda c, n: (c, 0))
    token_out = pl.BlockSpec((length, width), lambda c, n: (c, 0))
    anywhere = pl.BlockSpec(memory_space=pl.ANY)

    def fixed(a):
        return pl.BlockSpec(a.shape, lambda c, n: (0, 0), pipeline_mode=pl.Buffered(1))

    shape = jax.ShapeDtypeStruct
    return pl.pallas_call(
        functools.partial(attend_kernel, heads=heads, span=span, first=first),
        grid_spec=pltpu.PrefetchScalarGridSpec(
            num_scalar_prefetch=1,
            grid=(number,),
            in_specs=[piece] * 4 + [fixed(w), fixed(wt), token, token] + [anywhere] * len(after),
            out_specs=[token_out, token_out, whole] + [piece] * 4,
            scratch_shapes=[pltpu.VMEM((rows, 2 * width), BF16)],
        ),
        out_shape=[shape((number * length, width), BF16)] * 2
        + [shape((number * rows, 2 * width), BF16)]
        + [shape((number * rows, part), BF16)] * 4,
        compiler_params=pltpu.CompilerParams(vmem_limit_bytes=60 * MIB),
        cost_estimate=pl.CostEstimate(
            flops=number * 6_000_000_000, bytes_accessed=4_000_000, transcendentals=0
        ),
    )(counts, *pieces, w, wt, q, do, *after)


def weights_kernel(quarters, *refs, chunks):
    pieces, grads = refs[: 4 * chunks], refs[4 * chunks : 5 * chunks]
    out, turned = refs[-2:]
    part = pieces[0].shape[1]
    rows = pieces[0].shape[0]

    @pl.when(pl.program_id(0) == 0)
    def _():
        for c in range(chunks):
            for r in range(4):
                turned[r * part : (r + 1) * part, c * rows : (c + 1) * rows] = pieces[4 * c + r][...].T

    total = dot(turned[:, :rows], grads[0][...])
    for c in range(1, chunks):
        total += dot(turned[:, c * rows : (c + 1) * rows], grads[c][...])
    for r in range(4):
        at = pl.ds(pl.multiple_of(quarters[r] * part, part), part)
        out[at, :] = total[r * part : (r + 1) * part].astype(BF16)


def weights(quarters, pieces, grads, after):
    chunks = len(pieces)
    flat = [p for chunk in pieces for p in chunk]
    part = flat[0].shape[1]
    rows, columns = grads[0].shape
    total = rows * chunks
    block = 512

    def fixed(a):
        return pl.BlockSpec(a.shape, lambda c, n: (0, 0), pipeline_mode=pl.Buffered(1))

    return pl.pallas_call(
        functools.partial(weights_kernel, chunks=chunks),
        grid_spec=pltpu.PrefetchScalarGridSpec(
            num_scalar_prefetch=1,
            grid=(columns // block,),
            in_specs=[fixed(p) for p in flat]
            + [pl.BlockSpec((rows, block), lambda c, n: (0, c))] * chunks
            + [pl.BlockSpec(memory_space=pl.ANY)] * len(after),
            out_specs=pl.BlockSpec((4 * part, block), lambda c, n: (0, c)),
            scratch_shapes=[pltpu.VMEM((4 * part, total), BF16)],
        ),
        out_shape=jax.ShapeDtypeStruct((4 * part, columns), BF16),
        compiler_params=pltpu.CompilerParams(vmem_limit_bytes=60 * MIB),
        cost_estimate=pl.CostEstimate(
            flops=4 * 4 * part * total * columns, bytes_accessed=22_000_000, transcendentals=0
        ),
    )(quarters, *flat, *grads, *after)


def body(queries, slot_table, states, key_weight, value_weight, out_grad):
    devices = lax.axis_size("ctx")
    groups = lax.axis_size("tp")
    me = lax.axis_index("tp")
    stretches, neighbours = slot_table.shape
    slots, span, enc = states.shape
    capacity = 2
    places = devices * capacity
    part = enc // groups
    width = key_weight.shape[1]

    flat = slot_table.reshape(-1)
    live = flat >= 0
    owner = jnp.where(live, flat // slots, -1)
    count = flat.shape[0]
    order = jnp.arange(count)
    alike = (owner[:, None] == owner[None, :]) & (order[None, :] < order[:, None])
    rank = jnp.sum(alike.astype(jnp.int32), axis=1)
    place = jnp.where(live, owner * capacity + rank, -1)
    counts = jnp.sum(live.reshape(stretches, neighbours).astype(jnp.int32), axis=1)
    hit = place[:, None] == jnp.arange(places)[None, :]
    asked = jnp.sum(jnp.where(hit, (flat % slots + 1)[:, None], 0), axis=0) - 1
    source = jnp.sum(jnp.where(hit, order[:, None], 0), axis=0)
    wanted = lax.all_to_all(asked.reshape(devices, capacity), "ctx", 0, 0, tiled=True).reshape(-1)
    goes = wanted[None, :] == jnp.arange(slots)[:, None]
    landing = jnp.sum(jnp.where(goes, jnp.arange(places)[None, :], 0), axis=1)

    quarters = (me + jnp.array([0, groups - 1, 1, 2], jnp.int32)) % groups
    both = jnp.concatenate([key_weight, value_weight], axis=1)
    w = jnp.take(both.reshape(groups, part, 2 * width), quarters, axis=0, mode="clip")
    w = w.reshape(enc, 2 * width)
    wt = w.T

    mine = lax.dynamic_slice_in_dim(states, me * part, part, axis=2)
    picked = jnp.take(mine, jnp.maximum(wanted, 0), axis=0, mode="clip")
    arrived = lax.all_to_all(
        picked.reshape(devices, capacity, span, part), "ctx", 0, 0, tiled=True
    ).reshape(places, span, part)
    opening = jnp.repeat(place.reshape(stretches, neighbours)[:, :1], neighbours, axis=1)
    filled = jnp.where(live, place, opening.reshape(-1))

    def shift(by):
        return [(i, (i + by) % groups) for i in range(groups)]

    def permute(x, by):
        return lax.ppermute(x, "tp", shift(by))

    chunks = stretches // CHUNK
    here = CHUNK * neighbours
    owns = [
        jnp.take(arrived, filled[c * here : (c + 1) * here], axis=0, mode="clip").reshape(
            here * span, part
        )
        for c in range(chunks)
    ]

    def collect(own, after):
        if after:
            own, *_ = lax.optimization_barrier((own, *after))
        return [own, permute(own, 1), permute(own, -1), permute(own, 2)]

    pieces = [collect(owns[0], ())]
    after = ()
    done, summed = [], []
    got = ()
    for c in range(chunks):
        if c < chunks - 1:
            pieces.append(collect(owns[c + 1], pieces[-1][1:]))
        *tokens, p0, p1, p2, p3 = attend(
            counts, pieces[c], w, wt, queries, out_grad, after, c * CHUNK, CHUNK, span
        )
        done.append(tokens)
        p0, p1, p2, p3, *_ = lax.optimization_barrier((p0, p1, p2, p3, *pieces[-1][1:], *got))
        got = [p0, permute(p1, -1), permute(p2, 1), permute(p3, 2)]
        after = summed[-1:]
        total = sum(g.astype(F32) for g in got)
        summed.append(total.astype(BF16).reshape(here, span, part))
    attended, query_grad = (jnp.concatenate([t[i] for t in done], axis=0) for i in range(2))
    grads = [t[2] for t in done]

    terms = weights(quarters, pieces, grads, after)
    leaving = jnp.take(jnp.concatenate(summed, axis=0), source, axis=0, mode="clip")
    landed = lax.all_to_all(
        leaving.reshape(devices, capacity, span, part), "ctx", 0, 0, tiled=True
    ).reshape(places, span, part)
    states_grad = jnp.take(landed, landing, axis=0, mode="clip")
    terms, *_ = lax.optimization_barrier((terms, leaving))
    terms = lax.all_to_all(
        terms.reshape(devices, enc // devices, 2 * width), "ctx", 0, 0, tiled=True
    )
    weight_grads = jnp.sum(terms.astype(F32), axis=0)
    return (
        attended,
        query_grad,
        states_grad,
        weight_grads[:, :width],
        weight_grads[:, width:],
    )


def solution(mesh):
    in_specs = (
        P("ctx", "tp"),
        P("ctx", None),
        P("ctx", None, None),
        P(None, "tp"),
        P(None, "tp"),
        P("ctx", "tp"),
    )
    out_specs = (
        P("ctx", "tp"),
        P("ctx", "tp"),
        P("ctx", None, "tp"),
        P("ctx", "tp"),
        P("ctx", "tp"),
    )
    return jax.shard_map(body, mesh=mesh, in_specs=in_specs, out_specs=out_specs, check_vma=False)
```

```python
import functools

import jax
import jax.numpy as jnp
from jax import lax
from jax.experimental import pallas as pl
from jax.experimental.pallas import tpu as pltpu
from jax.sharding import PartitionSpec as P

HEAD_DIM = 128
CHUNK = 4
F32 = jnp.float32
BF16 = jnp.bfloat16
NN = (((1,), (0,)), ((), ()))
NT = (((1,), (1,)), ((), ()))
TN = (((0,), (0,)), ((), ()))
MIB = 2**20


def dot(a, b, dims=NN):
    return lax.dot_general(a, b, dims, preferred_element_type=F32)


def attend_kernel(
    counts, quarters, s0, s1, s2, s3, w, wt, q_ref, do_ref, *rest, heads, span, first, before, last
):
    att, qg, p0, p1, p2, p3, out, kv, grads, total = rest[-10:]
    c = pl.program_id(0)
    width = heads * HEAD_DIM
    scale = HEAD_DIM ** (-0.5)
    rows = s0.shape[0]
    length = q_ref.shape[0]
    states = jnp.concatenate([s0[...], s1[...], s2[...], s3[...]], axis=1)
    kv[...] = dot(states, w[...]).astype(BF16)
    mask = lax.broadcasted_iota(jnp.int32, (rows, 1), 0) < counts[first + c] * span
    zero = jnp.zeros((length, HEAD_DIM), BF16)

    def spread(ref, lo):
        top = jnp.concatenate([ref[:, lo : lo + HEAD_DIM], zero], axis=1)
        low = jnp.concatenate([zero, ref[:, lo + HEAD_DIM : lo + 2 * HEAD_DIM]], axis=1)
        return jnp.concatenate([top, low], axis=0)

    for h in range(0, heads, 2):
        lo = h * HEAD_DIM
        mid, hi = lo + HEAD_DIM, lo + 2 * HEAD_DIM
        q = spread(q_ref, lo)
        do = spread(do_ref, lo)
        k = kv[:, lo:hi]
        v = kv[:, width + lo : width + hi]
        scores = jnp.where(mask, dot(k, q, NT), -jnp.inf)
        dprobs = dot(v, do, NT)
        expo = jnp.exp((scores - jnp.max(scores, axis=0, keepdims=True)) * scale)
        probs = expo * (1.0 / jnp.sum(expo, axis=0, keepdims=True))
        dscores = probs * (dprobs - jnp.sum(probs * dprobs, axis=0, keepdims=True))
        probs_b = probs.astype(BF16)
        dscores_b = dscores.astype(BF16)
        grads[:, width + lo : width + hi] = dot(probs_b, do).astype(BF16)
        grads[:, lo:hi] = (dot(dscores_b, q) * scale).astype(BF16)
        both = dot(probs_b, v, TN).astype(BF16)
        att[:, lo:mid] = both[:length, :HEAD_DIM]
        att[:, mid:hi] = both[length:, HEAD_DIM:]
        both = (dot(dscores_b, k, TN) * scale).astype(BF16)
        qg[:, lo:mid] = both[:length, :HEAD_DIM]
        qg[:, mid:hi] = both[length:, HEAD_DIM:]
    terms = dot(states, grads[...], TN)
    if before:
        total[...] = jnp.where(c == 0, rest[0][...], total[...]) + terms
    else:

        @pl.when(c == 0)
        def _():
            total[...] = terms

        @pl.when(c > 0)
        def _():
            total[...] += terms

    part = dot(grads[...], wt[...]).astype(BF16)
    n = p0.shape[1]
    p0[...] = part[:, :n]
    p1[...] = part[:, n : 2 * n]
    p2[...] = part[:, 2 * n : 3 * n]
    p3[...] = part[:, 3 * n :]

    @pl.when(c == pl.num_programs(0) - 1)
    def _():
        if not last:
            out[...] = total[...]
            return
        for r in range(4):
            at = pl.ds(pl.multiple_of(quarters[r] * n, n), n)
            out[at, :] = total[r * n : (r + 1) * n, :].astype(BF16)


def attend(counts, quarters, pieces, w, wt, q, do, terms, after, first, number, span):
    heads = q.shape[1] // HEAD_DIM
    stretches = counts.shape[0]
    length = q.shape[0] // stretches
    width = q.shape[1]
    rows = pieces[0].shape[0] // number
    part = pieces[0].shape[1]
    last = first + number == stretches
    piece = pl.BlockSpec((rows, part), lambda c, *_: (c, 0))
    token = pl.BlockSpec((length, width), lambda c, *_: (first + c, 0))
    token_out = pl.BlockSpec((length, width), lambda c, *_: (c, 0))
    anywhere = pl.BlockSpec(memory_space=pl.ANY)

    def fixed(a):
        return pl.BlockSpec(a.shape, lambda c, *_: (0, 0), pipeline_mode=pl.Buffered(1))

    shape = jax.ShapeDtypeStruct
    sums = shape(w.shape, BF16 if last else F32)
    return pl.pallas_call(
        functools.partial(
            attend_kernel, heads=heads, span=span, first=first, before=bool(terms), last=last
        ),
        grid_spec=pltpu.PrefetchScalarGridSpec(
            num_scalar_prefetch=2,
            grid=(number,),
            in_specs=[piece] * 4
            + [fixed(w), fixed(wt), token, token]
            + [fixed(t) for t in terms]
            + [anywhere] * len(after),
            out_specs=[token_out, token_out] + [piece] * 4 + [fixed(sums)],
            scratch_shapes=[
                pltpu.VMEM((rows, 2 * width), BF16),
                pltpu.VMEM((rows, 2 * width), BF16),
                pltpu.VMEM(w.shape, F32),
            ],
        ),
        out_shape=[shape((number * length, width), BF16)] * 2
        + [shape((number * rows, part), BF16)] * 4
        + [sums],
        compiler_params=pltpu.CompilerParams(vmem_limit_bytes=60 * MIB),
        cost_estimate=pl.CostEstimate(
            flops=number * 6_000_000_000, bytes_accessed=4_000_000, transcendentals=0
        ),
    )(counts, quarters, *pieces, w, wt, q, do, *terms, *after)


def merge_kernel(at, earlier, a, b, c, d, out, total):
    half = earlier.shape[0]
    total[:half] = earlier[...]
    whole = a[...].astype(F32) + b[...].astype(F32) + (c[...].astype(F32) + d[...].astype(F32))
    total[half:] = whole.astype(BF16).reshape(earlier.shape)
    for i in range(out.shape[0]):
        out[i] = total[at[i]]


def merge(at, earlier, last):
    half, span, part = earlier.shape
    shape = at.shape + (span, part)
    flat = pl.BlockSpec((half * span, part), lambda i, at: (0, 0))
    return pl.pallas_call(
        merge_kernel,
        grid_spec=pltpu.PrefetchScalarGridSpec(
            num_scalar_prefetch=1,
            grid=(1,),
            in_specs=[pl.BlockSpec(earlier.shape, lambda i, at: (0, 0, 0))] + [flat] * 4,
            out_specs=pl.BlockSpec(shape, lambda i, at: (0, 0, 0)),
            scratch_shapes=[pltpu.VMEM((2 * half, span, part), BF16)],
        ),
        out_shape=jax.ShapeDtypeStruct(shape, BF16),
        compiler_params=pltpu.CompilerParams(vmem_limit_bytes=24 * MIB),
        cost_estimate=pl.CostEstimate(flops=0, bytes_accessed=4_000_000, transcendentals=0),
    )(at, earlier, *last)


def body(queries, slot_table, states, key_weight, value_weight, out_grad):
    devices = lax.axis_size("ctx")
    groups = lax.axis_size("tp")
    me = lax.axis_index("tp")
    stretches, neighbours = slot_table.shape
    slots, span, enc = states.shape
    capacity = 2
    places = devices * capacity
    part = enc // groups
    width = key_weight.shape[1]

    flat = slot_table.reshape(-1)
    live = flat >= 0
    owner = jnp.where(live, flat // slots, -1)
    count = flat.shape[0]
    order = jnp.arange(count)
    alike = (owner[:, None] == owner[None, :]) & (order[None, :] < order[:, None])
    rank = jnp.sum(alike.astype(jnp.int32), axis=1)
    place = jnp.where(live, owner * capacity + rank, -1)
    counts = jnp.sum(live.reshape(stretches, neighbours).astype(jnp.int32), axis=1)
    hit = place[:, None] == jnp.arange(places)[None, :]
    asked = jnp.sum(jnp.where(hit, (flat % slots + 1)[:, None], 0), axis=0) - 1
    source = jnp.sum(jnp.where(hit, order[:, None], 0), axis=0)
    wanted = lax.all_to_all(asked.reshape(devices, capacity), "ctx", 0, 0, tiled=True).reshape(-1)
    goes = wanted[None, :] == jnp.arange(slots)[:, None]
    landing = jnp.sum(jnp.where(goes, jnp.arange(places)[None, :], 0), axis=1)

    quarters = (me + jnp.array([0, groups - 1, 1, 2], jnp.int32)) % groups
    both = jnp.concatenate([key_weight, value_weight], axis=1)
    w = jnp.take(both.reshape(groups, part, 2 * width), quarters, axis=0, mode="clip")
    w = w.reshape(enc, 2 * width)
    wt = w.T

    mine = lax.dynamic_slice_in_dim(states, me * part, part, axis=2)
    picked = jnp.take(mine, jnp.maximum(wanted, 0), axis=0, mode="clip")
    arrived = lax.all_to_all(
        picked.reshape(devices, capacity, span, part), "ctx", 0, 0, tiled=True
    ).reshape(places, span, part)
    opening = jnp.repeat(place.reshape(stretches, neighbours)[:, :1], neighbours, axis=1)
    filled = jnp.where(live, place, opening.reshape(-1))

    def shift(by):
        return [(i, (i + by) % groups) for i in range(groups)]

    def permute(x, by):
        return lax.ppermute(x, "tp", shift(by))

    chunks = stretches // CHUNK
    here = CHUNK * neighbours
    owns = [
        jnp.take(arrived, filled[c * here : (c + 1) * here], axis=0, mode="clip").reshape(
            here * span, part
        )
        for c in range(chunks)
    ]

    def collect(own, after):
        if after:
            own, *_ = lax.optimization_barrier((own, *after))
        return [own, permute(own, 1), permute(own, -1), permute(own, 2)]

    pieces = [collect(owns[0], ())]
    after, terms, got = (), (), ()
    done, summed = [], []
    for c in range(chunks):
        if c < chunks - 1:
            pieces.append(collect(owns[c + 1], pieces[-1][1:]))
        *tokens, p0, p1, p2, p3, sums = attend(
            counts, quarters, pieces[c], w, wt, queries, out_grad, terms, after, c * CHUNK, CHUNK, span
        )
        done.append(tokens)
        terms = (sums,)
        p0, p1, p2, p3, sums, *_ = lax.optimization_barrier(
            (p0, p1, p2, p3, sums, *pieces[-1][1:], *got)
        )
        far = permute(p3, 2)
        if c == chunks - 1:
            core = lax.axis_index("ctx") % 2
            shares = sums.reshape(devices // 2, 2, enc // devices, 2 * width)
            keep = lax.dynamic_index_in_dim(shares, core, 1, keepdims=False)
            send = lax.dynamic_index_in_dim(shares, 1 - core, 1, keepdims=False)
            found = lax.ppermute(send, "ctx", [(i, i ^ 1) for i in range(devices)])
            chip = (keep.astype(F32) + found.astype(F32)).astype(BF16)
            p1, p2, chip, far = lax.optimization_barrier((p1, p2, chip, far))
        got = [p0, permute(p1, -1), permute(p2, 1), far]
        after = summed[-1:]
        if c < chunks - 1:
            total = sum(g.astype(F32) for g in got)
            summed.append(total.astype(BF16).reshape(here, span, part))
    attended, query_grad = (jnp.concatenate([t[i] for t in done], axis=0) for i in range(2))

    same = [list(range(c, devices, 2)) for c in range(2)]
    chip = lax.all_to_all(chip, "ctx", 0, 0, axis_index_groups=same, tiled=True)
    weight_grads = jnp.sum(chip.astype(F32), axis=0)

    leaving = merge(source, jnp.concatenate(summed, axis=0), got)
    landed = lax.all_to_all(
        leaving.reshape(devices, capacity, span, part), "ctx", 0, 0, tiled=True
    ).reshape(places, span, part)
    states_grad = jnp.take(landed, landing, axis=0, mode="clip")
    return (
        attended,
        query_grad,
        states_grad,
        weight_grads[:, :width],
        weight_grads[:, width:],
    )


def solution(mesh):
    in_specs = (
        P("ctx", "tp"),
        P("ctx", None),
        P("ctx", None, None),
        P(None, "tp"),
        P(None, "tp"),
        P("ctx", "tp"),
    )
    out_specs = (
        P("ctx", "tp"),
        P("ctx", "tp"),
        P("ctx", None, "tp"),
        P("ctx", "tp"),
        P("ctx", "tp"),
    )
    return jax.shard_map(body, mesh=mesh, in_specs=in_specs, out_specs=out_specs, check_vma=False)
```

```python
import functools

import jax
import jax.numpy as jnp
from jax import lax
from jax.experimental import pallas as pl
from jax.experimental.pallas import tpu as pltpu
from jax.sharding import PartitionSpec as P

HEAD_DIM = 128
CHUNK = 4
F32 = jnp.float32
BF16 = jnp.bfloat16
NN = (((1,), (0,)), ((), ()))
NT = (((1,), (1,)), ((), ()))
TN = (((0,), (0,)), ((), ()))
MIB = 2**20


def dot(a, b, dims=NN):
    return lax.dot_general(a, b, dims, preferred_element_type=F32)


def attend_kernel(
    counts, quarters, s0, s1, s2, s3, w, wt, q_ref, do_ref, *rest, heads, span, first, before, last
):
    att, qg, p0, p1, p2, p3, out, kv, grads, total = rest[-10:]
    c = pl.program_id(0)
    width = heads * HEAD_DIM
    scale = HEAD_DIM ** (-0.5)
    length = q_ref.shape[0]
    zero = jnp.zeros((length, HEAD_DIM), BF16)
    live = counts[first + c]

    def spread(ref, lo):
        top = jnp.concatenate([ref[:, lo : lo + HEAD_DIM], zero], axis=1)
        low = jnp.concatenate([zero, ref[:, lo + HEAD_DIM : lo + 2 * HEAD_DIM]], axis=1)
        return jnp.concatenate([top, low], axis=0)

    def stretch(met):
        rows = met * span
        states = jnp.concatenate([s[:rows] for s in (s0, s1, s2, s3)], axis=1)
        kv[:rows] = dot(states, w[...]).astype(BF16)
        mask = lax.broadcasted_iota(jnp.int32, (rows, 1), 0) < live * span
        for h in range(0, heads, 2):
            lo = h * HEAD_DIM
            mid, hi = lo + HEAD_DIM, lo + 2 * HEAD_DIM
            q = spread(q_ref, lo)
            do = spread(do_ref, lo)
            k = kv[:rows, lo:hi]
            v = kv[:rows, width + lo : width + hi]
            scores = jnp.where(mask, dot(k, q, NT), -jnp.inf)
            dprobs = dot(v, do, NT)
            expo = jnp.exp((scores - jnp.max(scores, axis=0, keepdims=True)) * scale)
            probs = expo * (1.0 / jnp.sum(expo, axis=0, keepdims=True))
            dscores = probs * (dprobs - jnp.sum(probs * dprobs, axis=0, keepdims=True))
            probs_b = probs.astype(BF16)
            dscores_b = dscores.astype(BF16)
            grads[:rows, width + lo : width + hi] = dot(probs_b, do).astype(BF16)
            grads[:rows, lo:hi] = (dot(dscores_b, q) * scale).astype(BF16)
            both = dot(probs_b, v, TN).astype(BF16)
            att[:, lo:mid] = both[:length, :HEAD_DIM]
            att[:, mid:hi] = both[length:, HEAD_DIM:]
            both = (dot(dscores_b, k, TN) * scale).astype(BF16)
            qg[:, lo:mid] = both[:length, :HEAD_DIM]
            qg[:, mid:hi] = both[length:, HEAD_DIM:]
        terms = dot(states, grads[:rows], TN)
        if before:
            total[...] = jnp.where(c == 0, rest[0][...], total[...]) + terms
        else:

            @pl.when(c == 0)
            def _():
                total[...] = terms

            @pl.when(c > 0)
            def _():
                total[...] += terms

        part = dot(grads[:rows], wt[...]).astype(BF16)
        n = p0.shape[1]
        for r, p in enumerate((p0, p1, p2, p3)):
            p[:rows] = part[:, r * n : (r + 1) * n]

    most = s0.shape[0] // span
    for met in range(2, most + 1):
        here = live <= met if met == 2 else live == met
        pl.when(here)(functools.partial(stretch, met))

    @pl.when(c == pl.num_programs(0) - 1)
    def _():
        if not last:
            out[...] = total[...]
            return
        n = p0.shape[1]
        for r in range(4):
            at = pl.ds(pl.multiple_of(quarters[r] * n, n), n)
            out[at, :] = total[r * n : (r + 1) * n, :].astype(BF16)


def attend(counts, quarters, pieces, w, wt, q, do, terms, after, first, number, span):
    heads = q.shape[1] // HEAD_DIM
    stretches = counts.shape[0]
    length = q.shape[0] // stretches
    width = q.shape[1]
    rows = pieces[0].shape[0] // number
    part = pieces[0].shape[1]
    last = first + number == stretches
    piece = pl.BlockSpec((rows, part), lambda c, *_: (c, 0))
    token = pl.BlockSpec((length, width), lambda c, *_: (first + c, 0))
    token_out = pl.BlockSpec((length, width), lambda c, *_: (c, 0))
    anywhere = pl.BlockSpec(memory_space=pl.ANY)

    def fixed(a):
        return pl.BlockSpec(a.shape, lambda c, *_: (0, 0), pipeline_mode=pl.Buffered(1))

    shape = jax.ShapeDtypeStruct
    sums = shape(w.shape, BF16 if last else F32)
    return pl.pallas_call(
        functools.partial(
            attend_kernel, heads=heads, span=span, first=first, before=bool(terms), last=last
        ),
        grid_spec=pltpu.PrefetchScalarGridSpec(
            num_scalar_prefetch=2,
            grid=(number,),
            in_specs=[piece] * 4
            + [fixed(w), fixed(wt), token, token]
            + [fixed(t) for t in terms]
            + [anywhere] * len(after),
            out_specs=[token_out, token_out] + [piece] * 4 + [fixed(sums)],
            scratch_shapes=[
                pltpu.VMEM((rows, 2 * width), BF16),
                pltpu.VMEM((rows, 2 * width), BF16),
                pltpu.VMEM(w.shape, F32),
            ],
        ),
        out_shape=[shape((number * length, width), BF16)] * 2
        + [shape((number * rows, part), BF16)] * 4
        + [sums],
        compiler_params=pltpu.CompilerParams(vmem_limit_bytes=60 * MIB),
        cost_estimate=pl.CostEstimate(
            flops=number * 6_000_000_000, bytes_accessed=4_000_000, transcendentals=0
        ),
    )(counts, quarters, *pieces, w, wt, q, do, *terms, *after)


def pick_kernel(at, source, out):
    for i in range(out.shape[0]):
        out[i] = source[at[i]]


def pick(at, states, quarter, part):
    slots, span, _ = states.shape
    shape = at.shape + (span, part)
    at = jnp.concatenate([at, quarter.reshape(1)])
    return pl.pallas_call(
        pick_kernel,
        grid_spec=pltpu.PrefetchScalarGridSpec(
            num_scalar_prefetch=1,
            grid=(1,),
            in_specs=[pl.BlockSpec((slots, span, part), lambda i, at: (0, 0, at[shape[0]]))],
            out_specs=pl.BlockSpec(shape, lambda i, at: (0, 0, 0)),
        ),
        out_shape=jax.ShapeDtypeStruct(shape, states.dtype),
        compiler_params=pltpu.CompilerParams(vmem_limit_bytes=60 * MIB),
        cost_estimate=pl.CostEstimate(flops=0, bytes_accessed=4_000_000, transcendentals=0),
    )(at, states)


def merge_kernel(at, earlier, a, b, c, d, out, total):
    half = earlier.shape[0]
    total[:half] = earlier[...]
    whole = a[...].astype(F32) + b[...].astype(F32) + (c[...].astype(F32) + d[...].astype(F32))
    total[half:] = whole.astype(BF16).reshape(earlier.shape)
    for i in range(out.shape[0]):
        out[i] = total[at[i]]


def merge(at, earlier, last):
    half, span, part = earlier.shape
    shape = at.shape + (span, part)
    flat = pl.BlockSpec((half * span, part), lambda i, at: (0, 0))
    return pl.pallas_call(
        merge_kernel,
        grid_spec=pltpu.PrefetchScalarGridSpec(
            num_scalar_prefetch=1,
            grid=(1,),
            in_specs=[pl.BlockSpec(earlier.shape, lambda i, at: (0, 0, 0))] + [flat] * 4,
            out_specs=pl.BlockSpec(shape, lambda i, at: (0, 0, 0)),
            scratch_shapes=[pltpu.VMEM((2 * half, span, part), BF16)],
        ),
        out_shape=jax.ShapeDtypeStruct(shape, BF16),
        compiler_params=pltpu.CompilerParams(vmem_limit_bytes=24 * MIB),
        cost_estimate=pl.CostEstimate(flops=0, bytes_accessed=4_000_000, transcendentals=0),
    )(at, earlier, *last)


def body(queries, slot_table, states, key_weight, value_weight, out_grad):
    devices = lax.axis_size("ctx")
    groups = lax.axis_size("tp")
    me = lax.axis_index("tp")
    stretches, neighbours = slot_table.shape
    slots, span, enc = states.shape
    capacity = 2
    places = devices * capacity
    part = enc // groups
    width = key_weight.shape[1]

    flat = slot_table.reshape(-1)
    live = flat >= 0
    owner = jnp.where(live, flat // slots, -1)
    count = flat.shape[0]
    order = jnp.arange(count)
    alike = (owner[:, None] == owner[None, :]) & (order[None, :] < order[:, None])
    rank = jnp.sum(alike.astype(jnp.int32), axis=1)
    place = jnp.where(live, owner * capacity + rank, -1)
    counts = jnp.sum(live.reshape(stretches, neighbours).astype(jnp.int32), axis=1)
    hit = place[:, None] == jnp.arange(places)[None, :]
    asked = jnp.sum(jnp.where(hit, (flat % slots + 1)[:, None], 0), axis=0) - 1
    source = jnp.sum(jnp.where(hit, order[:, None], 0), axis=0)
    wanted = lax.all_to_all(asked.reshape(devices, capacity), "ctx", 0, 0, tiled=True).reshape(-1)
    goes = wanted[None, :] == jnp.arange(slots)[:, None]
    landing = jnp.sum(jnp.where(goes, jnp.arange(places)[None, :], 0), axis=1)

    quarters = (me + jnp.array([0, groups - 1, 1, 2], jnp.int32)) % groups
    both = jnp.concatenate([key_weight, value_weight], axis=1)
    w = jnp.take(both.reshape(groups, part, 2 * width), quarters, axis=0, mode="clip")
    w = w.reshape(enc, 2 * width)
    wt = w.T

    picked = pick(jnp.maximum(wanted, 0), states, me, part)
    arrived = lax.all_to_all(
        picked.reshape(devices, capacity, span, part), "ctx", 0, 0, tiled=True
    ).reshape(places, span, part)
    opening = jnp.repeat(place.reshape(stretches, neighbours)[:, :1], neighbours, axis=1)
    filled = jnp.where(live, place, opening.reshape(-1))

    def shift(by):
        return [(i, (i + by) % groups) for i in range(groups)]

    def permute(x, by):
        return lax.ppermute(x, "tp", shift(by))

    chunks = stretches // CHUNK
    here = CHUNK * neighbours
    owns = [
        jnp.take(arrived, filled[c * here : (c + 1) * here], axis=0, mode="clip").reshape(
            here * span, part
        )
        for c in range(chunks)
    ]

    def collect(own, after):
        if after:
            own, *_ = lax.optimization_barrier((own, *after))
        return [own, permute(own, 1), permute(own, -1), permute(own, 2)]

    pieces = [collect(owns[0], ())]
    after, terms, got = (), (), ()
    done, summed = [], []
    for c in range(chunks):
        if c < chunks - 1:
            pieces.append(collect(owns[c + 1], pieces[-1][1:]))
        *tokens, p0, p1, p2, p3, sums = attend(
            counts, quarters, pieces[c], w, wt, queries, out_grad, terms, after, c * CHUNK, CHUNK, span
        )
        done.append(tokens)
        terms = (sums,)
        p0, p1, p2, p3, sums, *_ = lax.optimization_barrier(
            (p0, p1, p2, p3, sums, *pieces[-1][1:], *got)
        )
        far = permute(p3, 2)
        if c == chunks - 1:
            core = lax.axis_index("ctx") % 2
            shares = sums.reshape(devices // 2, 2, enc // devices, 2 * width)
            keep = lax.dynamic_index_in_dim(shares, core, 1, keepdims=False)
            send = lax.dynamic_index_in_dim(shares, 1 - core, 1, keepdims=False)
            found = lax.ppermute(send, "ctx", [(i, i ^ 1) for i in range(devices)])
            chip = (keep.astype(F32) + found.astype(F32)).astype(BF16)
            p1, p2, chip, far = lax.optimization_barrier((p1, p2, chip, far))
        got = [p0, permute(p1, -1), permute(p2, 1), far]
        after = summed[-1:]
        if c < chunks - 1:
            total = sum(g.astype(F32) for g in got)
            summed.append(total.astype(BF16).reshape(here, span, part))
    attended, query_grad = (jnp.concatenate([t[i] for t in done], axis=0) for i in range(2))

    same = [list(range(c, devices, 2)) for c in range(2)]
    chip = lax.all_to_all(chip, "ctx", 0, 0, axis_index_groups=same, tiled=True)
    weight_grads = jnp.sum(chip.astype(F32), axis=0)

    leaving = merge(source, jnp.concatenate(summed, axis=0), got)
    landed = lax.all_to_all(
        leaving.reshape(devices, capacity, span, part), "ctx", 0, 0, tiled=True
    ).reshape(places, span, part)
    states_grad = jnp.take(landed, landing, axis=0, mode="clip")
    return (
        attended,
        query_grad,
        states_grad,
        weight_grads[:, :width],
        weight_grads[:, width:],
    )


def solution(mesh):
    in_specs = (
        P("ctx", "tp"),
        P("ctx", None),
        P("ctx", None, None),
        P(None, "tp"),
        P(None, "tp"),
        P("ctx", "tp"),
    )
    out_specs = (
        P("ctx", "tp"),
        P("ctx", "tp"),
        P("ctx", None, "tp"),
        P("ctx", "tp"),
        P("ctx", "tp"),
    )
    return jax.shard_map(body, mesh=mesh, in_specs=in_specs, out_specs=out_specs, check_vma=False)
```

```python
import functools

import jax
import jax.numpy as jnp
from jax import lax
from jax.experimental import pallas as pl
from jax.experimental.pallas import tpu as pltpu
from jax.sharding import PartitionSpec as P

HEAD_DIM = 128
CHUNK = 4
F32 = jnp.float32
BF16 = jnp.bfloat16
NN = (((1,), (0,)), ((), ()))
NT = (((1,), (1,)), ((), ()))
TN = (((0,), (0,)), ((), ()))
MIB = 2**20


def dot(a, b, dims=NN):
    return lax.dot_general(a, b, dims, preferred_element_type=F32)


def attend_kernel(
    counts, quarters, s0, s1, s2, s3, w, wt, q_ref, do_ref, *rest, heads, span, first, before, last
):
    att, qg, p0, p1, p2, p3, out, kv, grads, total = rest[-10:]
    c = pl.program_id(0)
    width = heads * HEAD_DIM
    scale = HEAD_DIM ** (-0.5)
    length = q_ref.shape[0]
    zero = jnp.zeros((length, HEAD_DIM), BF16)
    live = counts[first + c]

    def spread(ref, lo):
        top = jnp.concatenate([ref[:, lo : lo + HEAD_DIM], zero], axis=1)
        low = jnp.concatenate([zero, ref[:, lo + HEAD_DIM : lo + 2 * HEAD_DIM]], axis=1)
        return jnp.concatenate([top, low], axis=0)

    def stretch(met):
        rows = met * span
        states = jnp.concatenate([s[:rows] for s in (s0, s1, s2, s3)], axis=1)
        kv[:rows] = dot(states, w[...]).astype(BF16)
        mask = lax.broadcasted_iota(jnp.int32, (rows, 1), 0) < live * span
        for h in range(0, heads, 2):
            lo = h * HEAD_DIM
            mid, hi = lo + HEAD_DIM, lo + 2 * HEAD_DIM
            q = spread(q_ref, lo)
            do = spread(do_ref, lo)
            k = kv[:rows, lo:hi]
            v = kv[:rows, width + lo : width + hi]
            scores = jnp.where(mask, dot(k, q, NT), -jnp.inf)
            dprobs = dot(v, do, NT)
            expo = jnp.exp((scores - jnp.max(scores, axis=0, keepdims=True)) * scale)
            probs = expo * (1.0 / jnp.sum(expo, axis=0, keepdims=True))
            dscores = probs * (dprobs - jnp.sum(probs * dprobs, axis=0, keepdims=True))
            probs_b = probs.astype(BF16)
            dscores_b = dscores.astype(BF16)
            grads[:rows, width + lo : width + hi] = dot(probs_b, do).astype(BF16)
            grads[:rows, lo:hi] = (dot(dscores_b, q) * scale).astype(BF16)
            both = dot(probs_b, v, TN).astype(BF16)
            att[:, lo:mid] = both[:length, :HEAD_DIM]
            att[:, mid:hi] = both[length:, HEAD_DIM:]
            both = (dot(dscores_b, k, TN) * scale).astype(BF16)
            qg[:, lo:mid] = both[:length, :HEAD_DIM]
            qg[:, mid:hi] = both[length:, HEAD_DIM:]
        terms = dot(states, grads[:rows], TN)
        if before:
            total[...] = jnp.where(c == 0, rest[0][...], total[...]) + terms
        else:

            @pl.when(c == 0)
            def _():
                total[...] = terms

            @pl.when(c > 0)
            def _():
                total[...] += terms

        part = dot(grads[:rows], wt[...]).astype(BF16)
        n = p0.shape[1]
        for r, p in enumerate((p0, p1, p2, p3)):
            p[:rows] = part[:, r * n : (r + 1) * n]

    most = s0.shape[0] // span
    if not before:
        stretch(most)
        cases = ()
    else:
        cases = range(2, most + 1)
    for met in cases:
        here = live <= met if met == 2 else live == met
        pl.when(here)(functools.partial(stretch, met))

    @pl.when(c == pl.num_programs(0) - 1)
    def _():
        if not last:
            out[...] = total[...]
            return
        n = p0.shape[1]
        for r in range(4):
            at = pl.ds(pl.multiple_of(quarters[r] * n, n), n)
            out[at, :] = total[r * n : (r + 1) * n, :].astype(BF16)


def attend(counts, quarters, pieces, w, wt, q, do, terms, after, first, number, span):
    heads = q.shape[1] // HEAD_DIM
    stretches = counts.shape[0]
    length = q.shape[0] // stretches
    width = q.shape[1]
    rows = pieces[0].shape[0] // number
    part = pieces[0].shape[1]
    last = first + number == stretches
    piece = pl.BlockSpec((rows, part), lambda c, *_: (c, 0))
    token = pl.BlockSpec((length, width), lambda c, *_: (first + c, 0))
    token_out = pl.BlockSpec((length, width), lambda c, *_: (c, 0))
    anywhere = pl.BlockSpec(memory_space=pl.ANY)

    def fixed(a):
        return pl.BlockSpec(a.shape, lambda c, *_: (0, 0), pipeline_mode=pl.Buffered(1))

    shape = jax.ShapeDtypeStruct
    sums = shape(w.shape, BF16 if last else F32)
    return pl.pallas_call(
        functools.partial(
            attend_kernel, heads=heads, span=span, first=first, before=bool(terms), last=last
        ),
        grid_spec=pltpu.PrefetchScalarGridSpec(
            num_scalar_prefetch=2,
            grid=(number,),
            in_specs=[piece] * 4
            + [fixed(w), fixed(wt), token, token]
            + [fixed(t) for t in terms]
            + [anywhere] * len(after),
            out_specs=[token_out, token_out] + [piece] * 4 + [fixed(sums)],
            scratch_shapes=[
                pltpu.VMEM((rows, 2 * width), BF16),
                pltpu.VMEM((rows, 2 * width), BF16),
                pltpu.VMEM(w.shape, F32),
            ],
        ),
        out_shape=[shape((number * length, width), BF16)] * 2
        + [shape((number * rows, part), BF16)] * 4
        + [sums],
        compiler_params=pltpu.CompilerParams(vmem_limit_bytes=60 * MIB),
        cost_estimate=pl.CostEstimate(
            flops=number * 6_000_000_000, bytes_accessed=4_000_000, transcendentals=0
        ),
    )(counts, quarters, *pieces, w, wt, q, do, *terms, *after)


def pick_kernel(at, source, out):
    for i in range(out.shape[0]):
        out[i] = source[at[i]]


def pick(at, states, quarter, part):
    slots, span, _ = states.shape
    shape = at.shape + (span, part)
    at = jnp.concatenate([at, quarter.reshape(1)])
    return pl.pallas_call(
        pick_kernel,
        grid_spec=pltpu.PrefetchScalarGridSpec(
            num_scalar_prefetch=1,
            grid=(1,),
            in_specs=[pl.BlockSpec((slots, span, part), lambda i, at: (0, 0, at[shape[0]]))],
            out_specs=pl.BlockSpec(shape, lambda i, at: (0, 0, 0)),
        ),
        out_shape=jax.ShapeDtypeStruct(shape, states.dtype),
        compiler_params=pltpu.CompilerParams(vmem_limit_bytes=60 * MIB),
        cost_estimate=pl.CostEstimate(flops=0, bytes_accessed=4_000_000, transcendentals=0),
    )(at, states)


def merge_kernel(at, earlier, a, b, c, d, out, total):
    half = earlier.shape[0]
    total[:half] = earlier[...]
    whole = a[...].astype(F32) + b[...].astype(F32) + (c[...].astype(F32) + d[...].astype(F32))
    total[half:] = whole.astype(BF16).reshape(earlier.shape)
    for i in range(out.shape[0]):
        out[i] = total[at[i]]


def merge(at, earlier, last):
    half, span, part = earlier.shape
    shape = at.shape + (span, part)
    flat = pl.BlockSpec((half * span, part), lambda i, at: (0, 0))
    return pl.pallas_call(
        merge_kernel,
        grid_spec=pltpu.PrefetchScalarGridSpec(
            num_scalar_prefetch=1,
            grid=(1,),
            in_specs=[pl.BlockSpec(earlier.shape, lambda i, at: (0, 0, 0))] + [flat] * 4,
            out_specs=pl.BlockSpec(shape, lambda i, at: (0, 0, 0)),
            scratch_shapes=[pltpu.VMEM((2 * half, span, part), BF16)],
        ),
        out_shape=jax.ShapeDtypeStruct(shape, BF16),
        compiler_params=pltpu.CompilerParams(vmem_limit_bytes=24 * MIB),
        cost_estimate=pl.CostEstimate(flops=0, bytes_accessed=4_000_000, transcendentals=0),
    )(at, earlier, *last)


def body(queries, slot_table, states, key_weight, value_weight, out_grad):
    devices = lax.axis_size("ctx")
    groups = lax.axis_size("tp")
    me = lax.axis_index("tp")
    stretches, neighbours = slot_table.shape
    slots, span, enc = states.shape
    capacity = 2
    places = devices * capacity
    part = enc // groups
    width = key_weight.shape[1]

    flat = slot_table.reshape(-1)
    live = flat >= 0
    owner = jnp.where(live, flat // slots, -1)
    count = flat.shape[0]
    order = jnp.arange(count)
    alike = (owner[:, None] == owner[None, :]) & (order[None, :] < order[:, None])
    rank = jnp.sum(alike.astype(jnp.int32), axis=1)
    place = jnp.where(live, owner * capacity + rank, -1)
    counts = jnp.sum(live.reshape(stretches, neighbours).astype(jnp.int32), axis=1)
    hit = place[:, None] == jnp.arange(places)[None, :]
    asked = jnp.sum(jnp.where(hit, (flat % slots + 1)[:, None], 0), axis=0) - 1
    source = jnp.sum(jnp.where(hit, order[:, None], 0), axis=0)
    wanted = lax.all_to_all(asked.reshape(devices, capacity), "ctx", 0, 0, tiled=True).reshape(-1)
    goes = wanted[None, :] == jnp.arange(slots)[:, None]
    landing = jnp.sum(jnp.where(goes, jnp.arange(places)[None, :], 0), axis=1)

    quarters = (me + jnp.array([0, groups - 1, 1, 2], jnp.int32)) % groups
    both = jnp.concatenate([key_weight, value_weight], axis=1)
    w = jnp.take(both.reshape(groups, part, 2 * width), quarters, axis=0, mode="clip")
    w = w.reshape(enc, 2 * width)
    wt = w.T

    picked = pick(jnp.maximum(wanted, 0), states, me, part)
    arrived = lax.all_to_all(
        picked.reshape(devices, capacity, span, part), "ctx", 0, 0, tiled=True
    ).reshape(places, span, part)
    opening = jnp.repeat(place.reshape(stretches, neighbours)[:, :1], neighbours, axis=1)
    filled = jnp.where(live, place, opening.reshape(-1))

    def shift(by):
        return [(i, (i + by) % groups) for i in range(groups)]

    def permute(x, by):
        return lax.ppermute(x, "tp", shift(by))

    chunks = stretches // CHUNK
    here = CHUNK * neighbours
    owns = [
        jnp.take(arrived, filled[c * here : (c + 1) * here], axis=0, mode="clip").reshape(
            here * span, part
        )
        for c in range(chunks)
    ]

    def collect(own, after):
        if after:
            own, *_ = lax.optimization_barrier((own, *after))
        return [own, permute(own, 1), permute(own, -1), permute(own, 2)]

    pieces = [collect(owns[0], ())]
    after, terms, got = (), (), ()
    done, summed = [], []
    for c in range(chunks):
        if c < chunks - 1:
            pieces.append(collect(owns[c + 1], pieces[-1][1:]))
        *tokens, p0, p1, p2, p3, sums = attend(
            counts, quarters, pieces[c], w, wt, queries, out_grad, terms, after, c * CHUNK, CHUNK, span
        )
        done.append(tokens)
        terms = (sums,)
        p0, p1, p2, p3, sums, *_ = lax.optimization_barrier(
            (p0, p1, p2, p3, sums, *pieces[-1][1:], *got)
        )
        far = permute(p3, 2)
        if c == chunks - 1:
            core = lax.axis_index("ctx") % 2
            shares = sums.reshape(devices // 2, 2, enc // devices, 2 * width)
            keep = lax.dynamic_index_in_dim(shares, core, 1, keepdims=False)
            send = lax.dynamic_index_in_dim(shares, 1 - core, 1, keepdims=False)
            found = lax.ppermute(send, "ctx", [(i, i ^ 1) for i in range(devices)])
            chip = (keep.astype(F32) + found.astype(F32)).astype(BF16)
            p1, p2, chip, far = lax.optimization_barrier((p1, p2, chip, far))
        got = [p0, permute(p1, -1), permute(p2, 1), far]
        after = summed[-1:]
        if c < chunks - 1:
            total = sum(g.astype(F32) for g in got)
            summed.append(total.astype(BF16).reshape(here, span, part))
    attended, query_grad = (jnp.concatenate([t[i] for t in done], axis=0) for i in range(2))

    same = [list(range(c, devices, 2)) for c in range(2)]
    chip = lax.all_to_all(chip, "ctx", 0, 0, axis_index_groups=same, tiled=True)
    weight_grads = jnp.sum(chip.astype(F32), axis=0)

    leaving = merge(source, jnp.concatenate(summed, axis=0), got)
    landed = lax.all_to_all(
        leaving.reshape(devices, capacity, span, part), "ctx", 0, 0, tiled=True
    ).reshape(places, span, part)
    states_grad = jnp.take(landed, landing, axis=0, mode="clip")
    return (
        attended,
        query_grad,
        states_grad,
        weight_grads[:, :width],
        weight_grads[:, width:],
    )


def solution(mesh):
    in_specs = (
        P("ctx", "tp"),
        P("ctx", None),
        P("ctx", None, None),
        P(None, "tp"),
        P(None, "tp"),
        P("ctx", "tp"),
    )
    out_specs = (
        P("ctx", "tp"),
        P("ctx", "tp"),
        P("ctx", None, "tp"),
        P("ctx", "tp"),
        P("ctx", "tp"),
    )
    return jax.shard_map(body, mesh=mesh, in_specs=in_specs, out_specs=out_specs, check_vma=False)
```

```python
import functools

import jax
import jax.numpy as jnp
from jax import lax
from jax.experimental import pallas as pl
from jax.experimental.pallas import tpu as pltpu
from jax.sharding import PartitionSpec as P

HEAD_DIM = 128
CHUNK = 4
F32 = jnp.float32
BF16 = jnp.bfloat16
NN = (((1,), (0,)), ((), ()))
NT = (((1,), (1,)), ((), ()))
TN = (((0,), (0,)), ((), ()))
MIB = 2**20


def dot(a, b, dims=NN):
    return lax.dot_general(a, b, dims, preferred_element_type=F32)


def attend_kernel(
    counts, quarters, s0, s1, s2, s3, w, q_ref, do_ref, *rest, heads, span, first, before, last
):
    att, qg, p0, p1, p2, p3, out, kv, grads, total = rest[-10:]
    c = pl.program_id(0)
    width = heads * HEAD_DIM
    scale = HEAD_DIM ** (-0.5)
    length = q_ref.shape[0]
    zero = jnp.zeros((length, HEAD_DIM), BF16)
    live = counts[first + c]

    def spread(ref, lo):
        top = jnp.concatenate([ref[:, lo : lo + HEAD_DIM], zero], axis=1)
        low = jnp.concatenate([zero, ref[:, lo + HEAD_DIM : lo + 2 * HEAD_DIM]], axis=1)
        return jnp.concatenate([top, low], axis=0)

    def stretch(met):
        rows = met * span
        states = jnp.concatenate([s[:rows] for s in (s0, s1, s2, s3)], axis=1)
        kv[:rows] = dot(states, w[...]).astype(BF16)
        mask = lax.broadcasted_iota(jnp.int32, (rows, 1), 0) < live * span
        for h in range(0, heads, 2):
            lo = h * HEAD_DIM
            mid, hi = lo + HEAD_DIM, lo + 2 * HEAD_DIM
            q = spread(q_ref, lo)
            do = spread(do_ref, lo)
            k = kv[:rows, lo:hi]
            v = kv[:rows, width + lo : width + hi]
            scores = jnp.where(mask, dot(k, q, NT), -jnp.inf)
            dprobs = dot(v, do, NT)
            expo = jnp.exp((scores - jnp.max(scores, axis=0, keepdims=True)) * scale)
            probs = expo * (1.0 / jnp.sum(expo, axis=0, keepdims=True))
            dscores = probs * (dprobs - jnp.sum(probs * dprobs, axis=0, keepdims=True))
            probs_b = probs.astype(BF16)
            dscores_b = dscores.astype(BF16)
            grads[:rows, width + lo : width + hi] = dot(probs_b, do).astype(BF16)
            grads[:rows, lo:hi] = (dot(dscores_b, q) * scale).astype(BF16)
            both = dot(probs_b, v, TN).astype(BF16)
            att[:, lo:mid] = both[:length, :HEAD_DIM]
            att[:, mid:hi] = both[length:, HEAD_DIM:]
            both = (dot(dscores_b, k, TN) * scale).astype(BF16)
            qg[:, lo:mid] = both[:length, :HEAD_DIM]
            qg[:, mid:hi] = both[length:, HEAD_DIM:]
        terms = dot(states, grads[:rows], TN)
        if before:
            total[...] = jnp.where(c == 0, rest[0][...], total[...]) + terms
        else:

            @pl.when(c == 0)
            def _():
                total[...] = terms

            @pl.when(c > 0)
            def _():
                total[...] += terms

        part = dot(grads[:rows], w[...], NT).astype(BF16)
        n = p0.shape[1]
        for r, p in enumerate((p0, p1, p2, p3)):
            p[:rows] = part[:, r * n : (r + 1) * n]

    most = s0.shape[0] // span
    if not before:
        stretch(most)
        cases = ()
    else:
        cases = range(2, most + 1)
    for met in cases:
        here = live <= met if met == 2 else live == met
        pl.when(here)(functools.partial(stretch, met))

    @pl.when(c == pl.num_programs(0) - 1)
    def _():
        if not last:
            out[...] = total[...]
            return
        n = p0.shape[1]
        for r in range(4):
            at = pl.ds(pl.multiple_of(quarters[r] * n, n), n)
            out[at, :] = total[r * n : (r + 1) * n, :].astype(BF16)


def attend(counts, quarters, pieces, w, q, do, terms, after, first, number, span):
    heads = q.shape[1] // HEAD_DIM
    stretches = counts.shape[0]
    length = q.shape[0] // stretches
    width = q.shape[1]
    rows = pieces[0].shape[0] // number
    part = pieces[0].shape[1]
    last = first + number == stretches
    piece = pl.BlockSpec((rows, part), lambda c, *_: (c, 0))
    token = pl.BlockSpec((length, width), lambda c, *_: (first + c, 0))
    token_out = pl.BlockSpec((length, width), lambda c, *_: (c, 0))
    anywhere = pl.BlockSpec(memory_space=pl.ANY)

    def fixed(a):
        return pl.BlockSpec(a.shape, lambda c, *_: (0, 0), pipeline_mode=pl.Buffered(1))

    shape = jax.ShapeDtypeStruct
    sums = shape(w.shape, BF16 if last else F32)
    return pl.pallas_call(
        functools.partial(
            attend_kernel, heads=heads, span=span, first=first, before=bool(terms), last=last
        ),
        grid_spec=pltpu.PrefetchScalarGridSpec(
            num_scalar_prefetch=2,
            grid=(number,),
            in_specs=[piece] * 4
            + [fixed(w), token, token]
            + [fixed(t) for t in terms]
            + [anywhere] * len(after),
            out_specs=[token_out, token_out] + [piece] * 4 + [fixed(sums)],
            scratch_shapes=[
                pltpu.VMEM((rows, 2 * width), BF16),
                pltpu.VMEM((rows, 2 * width), BF16),
                pltpu.VMEM(w.shape, F32),
            ],
        ),
        out_shape=[shape((number * length, width), BF16)] * 2
        + [shape((number * rows, part), BF16)] * 4
        + [sums],
        compiler_params=pltpu.CompilerParams(vmem_limit_bytes=60 * MIB),
        cost_estimate=pl.CostEstimate(
            flops=number * 6_000_000_000, bytes_accessed=4_000_000, transcendentals=0
        ),
    )(counts, quarters, *pieces, w, q, do, *terms, *after)


def pick_kernel(at, source, out):
    for i in range(out.shape[0]):
        out[i] = source[at[i]]


def pick(at, states, quarter, part):
    slots, span, _ = states.shape
    shape = at.shape + (span, part)
    at = jnp.concatenate([at, quarter.reshape(1)])
    return pl.pallas_call(
        pick_kernel,
        grid_spec=pltpu.PrefetchScalarGridSpec(
            num_scalar_prefetch=1,
            grid=(1,),
            in_specs=[pl.BlockSpec((slots, span, part), lambda i, at: (0, 0, at[shape[0]]))],
            out_specs=pl.BlockSpec(shape, lambda i, at: (0, 0, 0)),
        ),
        out_shape=jax.ShapeDtypeStruct(shape, states.dtype),
        compiler_params=pltpu.CompilerParams(vmem_limit_bytes=60 * MIB),
        cost_estimate=pl.CostEstimate(flops=0, bytes_accessed=4_000_000, transcendentals=0),
    )(at, states)


def merge_kernel(at, earlier, a, b, c, d, out, total):
    half = earlier.shape[0]
    total[:half] = earlier[...]
    whole = a[...].astype(F32) + b[...].astype(F32) + (c[...].astype(F32) + d[...].astype(F32))
    total[half:] = whole.astype(BF16).reshape(earlier.shape)
    for i in range(out.shape[0]):
        out[i] = total[at[i]]


def merge(at, earlier, last):
    half, span, part = earlier.shape
    shape = at.shape + (span, part)
    flat = pl.BlockSpec((half * span, part), lambda i, at: (0, 0))
    return pl.pallas_call(
        merge_kernel,
        grid_spec=pltpu.PrefetchScalarGridSpec(
            num_scalar_prefetch=1,
            grid=(1,),
            in_specs=[pl.BlockSpec(earlier.shape, lambda i, at: (0, 0, 0))] + [flat] * 4,
            out_specs=pl.BlockSpec(shape, lambda i, at: (0, 0, 0)),
            scratch_shapes=[pltpu.VMEM((2 * half, span, part), BF16)],
        ),
        out_shape=jax.ShapeDtypeStruct(shape, BF16),
        compiler_params=pltpu.CompilerParams(vmem_limit_bytes=24 * MIB),
        cost_estimate=pl.CostEstimate(flops=0, bytes_accessed=4_000_000, transcendentals=0),
    )(at, earlier, *last)


def body(queries, slot_table, states, key_weight, value_weight, out_grad):
    devices = lax.axis_size("ctx")
    groups = lax.axis_size("tp")
    me = lax.axis_index("tp")
    stretches, neighbours = slot_table.shape
    slots, span, enc = states.shape
    capacity = 2
    places = devices * capacity
    part = enc // groups
    width = key_weight.shape[1]

    flat = slot_table.reshape(-1)
    live = flat >= 0
    owner = jnp.where(live, flat // slots, -1)
    count = flat.shape[0]
    order = jnp.arange(count)
    alike = (owner[:, None] == owner[None, :]) & (order[None, :] < order[:, None])
    rank = jnp.sum(alike.astype(jnp.int32), axis=1)
    place = jnp.where(live, owner * capacity + rank, -1)
    counts = jnp.sum(live.reshape(stretches, neighbours).astype(jnp.int32), axis=1)
    hit = place[:, None] == jnp.arange(places)[None, :]
    asked = jnp.sum(jnp.where(hit, (flat % slots + 1)[:, None], 0), axis=0) - 1
    source = jnp.sum(jnp.where(hit, order[:, None], 0), axis=0)
    wanted = lax.all_to_all(asked.reshape(devices, capacity), "ctx", 0, 0, tiled=True).reshape(-1)
    goes = wanted[None, :] == jnp.arange(slots)[:, None]
    landing = jnp.sum(jnp.where(goes, jnp.arange(places)[None, :], 0), axis=1)

    quarters = (me + jnp.array([0, groups - 1, 1, 2], jnp.int32)) % groups
    both = jnp.concatenate([key_weight, value_weight], axis=1)
    w = jnp.take(both.reshape(groups, part, 2 * width), quarters, axis=0, mode="clip")
    w = w.reshape(enc, 2 * width)

    picked = pick(jnp.maximum(wanted, 0), states, me, part)
    arrived = lax.all_to_all(
        picked.reshape(devices, capacity, span, part), "ctx", 0, 0, tiled=True
    ).reshape(places, span, part)
    opening = jnp.repeat(place.reshape(stretches, neighbours)[:, :1], neighbours, axis=1)
    filled = jnp.where(live, place, opening.reshape(-1))

    def shift(by):
        return [(i, (i + by) % groups) for i in range(groups)]

    def permute(x, by):
        return lax.ppermute(x, "tp", shift(by))

    chunks = stretches // CHUNK
    here = CHUNK * neighbours
    owns = [
        jnp.take(arrived, filled[c * here : (c + 1) * here], axis=0, mode="clip").reshape(
            here * span, part
        )
        for c in range(chunks)
    ]

    def collect(own, after):
        if after:
            own, *_ = lax.optimization_barrier((own, *after))
        return [own, permute(own, 1), permute(own, -1), permute(own, 2)]

    pieces = [collect(owns[0], ())]
    after, terms, got = (), (), ()
    done, summed = [], []
    for c in range(chunks):
        if c < chunks - 1:
            pieces.append(collect(owns[c + 1], pieces[-1][1:]))
        *tokens, p0, p1, p2, p3, sums = attend(
            counts, quarters, pieces[c], w, queries, out_grad, terms, after, c * CHUNK, CHUNK, span
        )
        done.append(tokens)
        terms = (sums,)
        p0, p1, p2, p3, sums, *_ = lax.optimization_barrier(
            (p0, p1, p2, p3, sums, *pieces[-1][1:], *got)
        )
        far = permute(p3, 2)
        if c == chunks - 1:
            core = lax.axis_index("ctx") % 2
            shares = sums.reshape(devices // 2, 2, enc // devices, 2 * width)
            keep = lax.dynamic_index_in_dim(shares, core, 1, keepdims=False)
            send = lax.dynamic_index_in_dim(shares, 1 - core, 1, keepdims=False)
            found = lax.ppermute(send, "ctx", [(i, i ^ 1) for i in range(devices)])
            chip = (keep.astype(F32) + found.astype(F32)).astype(BF16)
        got = [p0, permute(p1, -1), permute(p2, 1), far]
        after = summed[-1:]
        if c < chunks - 1:
            total = sum(g.astype(F32) for g in got)
            summed.append(total.astype(BF16).reshape(here, span, part))
    attended, query_grad = (jnp.concatenate([t[i] for t in done], axis=0) for i in range(2))

    same = [list(range(c, devices, 2)) for c in range(2)]
    chip = lax.all_to_all(chip, "ctx", 0, 0, axis_index_groups=same, tiled=True)
    weight_grads = jnp.sum(chip.astype(F32), axis=0)

    leaving = merge(source, jnp.concatenate(summed, axis=0), got)
    landed = lax.all_to_all(
        leaving.reshape(devices, capacity, span, part), "ctx", 0, 0, tiled=True
    ).reshape(places, span, part)
    states_grad = jnp.take(landed, landing, axis=0, mode="clip")
    return (
        attended,
        query_grad,
        states_grad,
        weight_grads[:, :width],
        weight_grads[:, width:],
    )


def solution(mesh):
    in_specs = (
        P("ctx", "tp"),
        P("ctx", None),
        P("ctx", None, None),
        P(None, "tp"),
        P(None, "tp"),
        P("ctx", "tp"),
    )
    out_specs = (
        P("ctx", "tp"),
        P("ctx", "tp"),
        P("ctx", None, "tp"),
        P("ctx", "tp"),
        P("ctx", "tp"),
    )
    return jax.shard_map(body, mesh=mesh, in_specs=in_specs, out_specs=out_specs, check_vma=False)
```
